256 devices in a mesh: section: 2 (over z_lo), dp: 2 (over core), expert: 64 (over z_hi, x, y).
Axes of the slice: x: 4, y: 4, z: 8 (z_hi: 4, z_lo: 2; z = z_hi * 2 + z_lo), core: 2. Of those that a mesh axis runs over, the one named last changes fastest.
Arguments:
- grad_out: bfloat16 [2, 8192, 3584], P(None, ('dp', 'expert')), may hold values from -6 to 6
- layer_in: bfloat16 [2, 2, 8192, 3584], P('section', None, ('dp', 'expert')), may hold values from -6 to 6
- routes: int32 [2, 2, 8192, 2], P('section', None, ('dp', 'expert')), may hold values from 0 to 31, all different within a row; in each aligned block of 64 rows (0 to 63, 64 to 127, ..., all dimensions but the last counted through in order) at most 5 rows name the same one
- gates: float32 [2, 2, 8192, 2], P('section', None, ('dp', 'expert')), may hold values from 0.05 to 0.5
- w_up: bfloat16 [2, 64, 3584, 512], P('section', 'expert', 'dp'), may hold values from -0.09375 to 0.09375
- w_down: bfloat16 [2, 64, 512, 3584], P('section', 'expert', None, 'dp'), may hold values from -0.1875 to 0.1875
Outputs:
- grad_in: bfloat16 [2, 2, 8192, 3584], P('section', None, ('dp', 'expert'))
- grad_up: bfloat16 [2, 64, 3584, 512], P('section', 'expert', 'dp')
- grad_down: bfloat16 [2, 64, 512, 3584], P('section', 'expert', None, 'dp')
The draws below stay inside these ranges and needn't reach their ends.
Inputs may be any that keep to these rules, and one draw needn't show every extreme that they name: `routes`: each token names 2 different experts. In each device's block of 64 tokens of one section and micro-batch no expert is named by more than 5 tokens, a bound that some block reaches.
All inputs are finite; a program needn't handle non-finite values.
Results may differ from the reference program's by a relative error of at most 0.0075.
Values may be sent and summed in bfloat16 or wider, within the bound.
No kernel may reach another device: no remote copies, remote signals or barrier semaphores. Data moves between devices by JAX's collectives and lax.ppermute only.
A program may use at most 128 MiB of HBM per device.

```python
import math
import jax
import jax.numpy as jnp
import numpy as np
from jax import lax

D = 3584
FF = 1024
MB = 2
TOK_DEV = 64
TOPW = 2
EXPERTS = 32
CAP = 5
TOKENS = 8192
N_SECTION = 2
N_DP = 2


def steps_of(rng, extent, split, low, high):
    def one(dim, blocks):
        heights = jax.random.uniform(jax.random.fold_in(jax.random.fold_in(rng, 6), dim), (blocks,), jnp.float32, low / len(split), high / len(split))
        return jnp.repeat(jnp.exp(heights), extent[dim] // blocks).reshape((-1,) + (1,) * (len(extent) - dim - 1))

    gain = one(*split[0])
    for cut in split[1:]:
        gain = gain * one(*cut)
    return gain


def assign_block(key, own, number, rows, amount, top, limit, skew):
    sequence = jax.random.permutation(key, amount)
    crowded, usual = shares(amount, rows * top, limit, skew, True), shares(amount, rows * top, limit, skew, False)
    places = jnp.arange(amount)

    def named(sizes, rotation):
        used = int((sizes > 0).sum())
        fixed = max(1, used // 4)
        shifted = fixed + (places - fixed + rotation * (used - fixed)) % max(1, amount - fixed)
        return jnp.zeros((amount,), jnp.int32).at[sequence[jnp.where(places < fixed, places, shifted)]].set(jnp.asarray(sizes, jnp.int32))

    sizes = jnp.where(number % 4 == 0, named(crowded, number // 4), named(usual, number - number // 4 - 1))
    mixed = jax.random.permutation(jax.random.fold_in(own, 3), amount)
    source_of, taker = mixed[0:amount // 2 * 2:2], mixed[1:amount // 2 * 2:2]
    slack = jnp.minimum(sizes[source_of] - 1, limit - sizes[taker]) // 2
    slack = jnp.where((source_of == sequence[0]) | (taker == sequence[0]) | (sizes[taker] == 0), 0, jnp.maximum(slack, 0))
    shifted = jax.random.randint(jax.random.fold_in(own, 4), (amount // 2,), 0, 1 << 20) % (slack + 1)
    sizes = sizes.at[source_of].add(-shifted).at[taker].add(shifted)
    items = jnp.searchsorted(jnp.cumsum(sizes), jnp.arange(rows * top), side="right").astype(jnp.int32)
    grid = items.reshape(top, rows).T
    grid = grid[jax.random.permutation(jax.random.fold_in(own, 1), rows)]
    rotation = jax.random.randint(jax.random.fold_in(own, 2), (rows, 1), 0, top)
    return jnp.take_along_axis(grid, (jnp.arange(top)[None, :] + rotation) % top, axis=1)


def shares(count, total, limit, slope, full):
    loads = [(1 << 20) // math.isqrt(standing ** slope) + 1 for standing in range(1, count + 1)]
    largest = limit if full else min(limit, max(-(-total // count), total * loads[0] // sum(loads)))
    least = 1 if total - largest >= count - 1 else 0
    given, spare = [largest] + [least] * (count - 1), total - largest - least * (count - 1)
    while spare > 0:
        free = [i for i in range(1, count) if given[i] < largest] or [i for i in range(1, count) if given[i] < limit]
        mass, budget = sum([loads[i] for i in free]), spare
        for i in free:
            extra = min(limit - given[i], max(1, budget * loads[i] // mass), spare)
            given[i] = given[i] + extra
            spare = spare - extra
    return np.array(given)


def gaussian(key, dims, deviation, bound, cuts=(), kind=jnp.bfloat16):
    values = deviation * jax.random.normal(key, dims, jnp.float32)
    if cuts:
        values = values * steps_of(key, dims, cuts, -0.22, 0.18)
    return jnp.clip(values, -bound, bound).astype(kind)


def setup_inputs(seed: int = 0) -> dict:
    seeds = jax.random.split(jax.random.key(seed), 7)
    grad_out = gaussian(seeds[0], (MB, TOKENS, D), 1.0, 6.0, ((1, 128),))
    layer_in = gaussian(seeds[1], (N_SECTION, MB, TOKENS, D), 1.0, 6.0, ((0, 2), (2, 128)))
    routes_keys = jax.random.split(jax.random.fold_in(seeds[2], 1), N_SECTION * MB * TOKENS // TOK_DEV)
    routes_turns = jax.random.permutation(jax.random.fold_in(seeds[2], 3), N_SECTION * MB * TOKENS // TOK_DEV)
    routes = jax.vmap(lambda own, number: assign_block(jax.random.fold_in(seeds[2], 2), own, number, TOK_DEV, EXPERTS, TOPW, CAP, 2))(routes_keys, routes_turns).reshape((N_SECTION, MB, TOKENS, TOPW))
    gates = jnp.clip(jnp.exp(math.log(0.5) - 2.3025851 * jax.random.uniform(seeds[3], (N_SECTION, MB, TOKENS, TOPW), jnp.float32) ** steps_of(seeds[3], (N_SECTION, MB, TOKENS, TOPW), ((0, 2), (2, 128)), -0.2, 0.2)), 0.05, 0.5)
    w_up = gaussian(seeds[4], (N_SECTION, 2 * EXPERTS, D, FF // 2), D ** -0.5, 0.09375, ((0, 2), (1, 64), (2, 2)))
    w_down = gaussian(seeds[5], (N_SECTION, 2 * EXPERTS, FF // 2, D), FF ** -0.5, 0.1875, ((0, 2), (1, 64), (3, 2)))
    return dict(grad_out=grad_out, layer_in=layer_in, routes=routes, gates=gates, w_up=w_up, w_down=w_down)


def silu_grad(preact):
    sigmoid_value = jax.nn.sigmoid(preact)
    return sigmoid_value * (1.0 + preact * (1.0 - sigmoid_value))

def reference(grad_out, layer_in, routes, gates, w_up, w_down):
    blocks = TOKENS // TOK_DEV
    rows_expert = blocks * CAP
    half_ff = FF // 2
    expert_ids = jnp.arange(EXPERTS, dtype=jnp.int32)
    block_ids = (jnp.arange(TOKENS, dtype=jnp.int32) // TOK_DEV)[:, None]
    incoming = grad_out
    section_grads = [None] * N_SECTION
    up_grads = [None] * N_SECTION
    down_grads = [None] * N_SECTION
    for section_number in reversed(range(N_SECTION)):
        input_slots = []
        scaled_slots = []
        slot_lists = []
        for micro_number in range(MB):
            route_now = routes[section_number, micro_number]
            scaled = (gates[section_number, micro_number][:, :, None] * incoming[micro_number][:, None, :].astype(jnp.float32)).astype(jnp.bfloat16)
            onehot = (route_now[:, :, None] == expert_ids).astype(jnp.int32).reshape(blocks, TOK_DEV * TOPW, EXPERTS)
            before = jnp.cumsum(onehot, axis=1) - onehot
            position = lax.optimization_barrier(jnp.sum(before * onehot, axis=2)).reshape(TOKENS, TOPW)
            slot_index = (route_now * rows_expert + block_ids * CAP + position).reshape(-1).astype(jnp.int32)
            input_rows = jnp.broadcast_to(layer_in[section_number, micro_number][:, None, :], (TOKENS, TOPW, D)).reshape(-1, D)
            input_buffer = jnp.zeros((EXPERTS * rows_expert, D), jnp.bfloat16).at[slot_index].set(input_rows)
            scaled_buffer = jnp.zeros((EXPERTS * rows_expert, D), jnp.bfloat16).at[slot_index].set(scaled.reshape(-1, D))
            input_slots.append(input_buffer.reshape(EXPERTS, rows_expert, D))
            scaled_slots.append(scaled_buffer.reshape(EXPERTS, rows_expert, D))
            slot_lists.append(slot_index)
        inputs_all = jnp.stack(input_slots, axis=1)
        scaled_all = jnp.stack(scaled_slots, axis=1)
        up_pairs = w_up[section_number].reshape(EXPERTS, 2, D, half_ff)
        down_pairs = w_down[section_number].reshape(EXPERTS, 2, half_ff, D)

        def per_expert(operands):
            inputs_expert, scaled_expert, up_pair, down_pair = operands
            sums_all = []
            up_parts = [jnp.zeros((N_DP, D, half_ff), jnp.float32) for half_number in range(2)]
            down_parts = [jnp.zeros((N_DP, half_ff, D), jnp.float32) for half_number in range(2)]
            for micro_number in range(MB):
                rows_in = inputs_expert[micro_number]
                rows_scaled = scaled_expert[micro_number]
                pieces = []
                for half_number in range(2):
                    up_matrix = up_pair[half_number]
                    down_matrix = down_pair[half_number]
                    pre_act = jnp.dot(rows_in, up_matrix, preferred_element_type=jnp.float32)
                    activated = jax.nn.silu(pre_act).astype(jnp.bfloat16)
                    grad_act = jnp.dot(rows_scaled, down_matrix.T, preferred_element_type=jnp.float32)
                    grad_pre = (grad_act * silu_grad(pre_act)).astype(jnp.bfloat16)
                    up_parts[half_number] = up_parts[half_number] + jnp.einsum('prd,prf->pdf', rows_in.reshape(N_DP, -1, D).astype(jnp.float32), grad_pre.reshape(N_DP, -1, half_ff).astype(jnp.float32))
                    down_parts[half_number] = down_parts[half_number] + jnp.einsum('prf,prd->pfd', activated.reshape(N_DP, -1, half_ff).astype(jnp.float32), rows_scaled.reshape(N_DP, -1, D).astype(jnp.float32))
                    pieces.append(jnp.dot(grad_pre, up_matrix.T, preferred_element_type=jnp.float32).astype(jnp.bfloat16))
                stacked = lax.optimization_barrier(jnp.stack(pieces))
                sums_all.append(lax.optimization_barrier(jnp.sum(stacked.astype(jnp.float32), axis=0)).astype(jnp.bfloat16))
            up_round = lax.optimization_barrier(jnp.stack(up_parts).astype(jnp.bfloat16))
            down_round = lax.optimization_barrier(jnp.stack(down_parts).astype(jnp.bfloat16))
            up_final = lax.optimization_barrier(jnp.sum(up_round.astype(jnp.float32), axis=1)).astype(jnp.bfloat16)
            down_final = lax.optimization_barrier(jnp.sum(down_round.astype(jnp.float32), axis=1)).astype(jnp.bfloat16)
            return (jnp.stack(sums_all), up_final, down_final)
        sums, up_final, down_final = lax.map(per_expert, (inputs_all, scaled_all, up_pairs, down_pairs))
        produced_list = []
        for micro_number in range(MB):
            flat_sums = sums[:, micro_number].reshape(-1, D)
            gathered = flat_sums[slot_lists[micro_number]].reshape(TOKENS, TOPW, D).astype(jnp.float32)
            produced = (incoming[micro_number].astype(jnp.float32) + lax.optimization_barrier(jnp.sum(gathered, axis=1))).astype(jnp.bfloat16)
            produced_list.append(produced)
        section_grads[section_number] = jnp.stack(produced_list)
        incoming = section_grads[section_number]
        up_grads[section_number] = up_final.reshape(2 * EXPERTS, D, half_ff)
        down_grads[section_number] = down_final.reshape(2 * EXPERTS, half_ff, D)
    return (jnp.stack(section_grads), jnp.stack(up_grads), jnp.stack(down_grads))
```

```python
import functools

import jax
import jax.numpy as jnp
from jax import lax
from jax.experimental import pallas as pl
from jax.experimental.pallas import tpu as pltpu
from jax.sharding import Mesh, PartitionSpec as P

BF = jnp.bfloat16
F32 = jnp.float32
LANES = 128
GROUP = 16
VMEM_BYTES = 28 << 20
CAP = 5
PAIRED = ("pair", "half")
ROWS = GROUP * CAP
NT = (((1,), (1,)), ((), ()))


def vmem_call(body, outs, scratch=(), scalars=0):
    spec = pl.BlockSpec(memory_space=pltpu.VMEM)
    smem = pl.BlockSpec(memory_space=pltpu.SMEM)

    def call(*args):
        return pl.pallas_call(
            body,
            out_shape=outs,
            in_specs=[smem] * scalars + [spec] * (len(args) - scalars),
            out_specs=jax.tree.map(lambda _: spec, outs),
            scratch_shapes=list(scratch),
            cost_estimate=pl.CostEstimate(flops=1, bytes_accessed=1, transcendentals=0),
            compiler_params=pltpu.CompilerParams(vmem_limit_bytes=VMEM_BYTES),
        )(*args)

    return call


def dot(a, b, dims=(((1,), (0,)), ((), ()))):
    return lax.dot_general(a, b, dims, preferred_element_type=F32)


def pack(source, starts, pack_ref, mixed, store):
    blocks = mixed.shape[0] // ROWS
    for side, (row, col) in enumerate(starts):
        for block in range(blocks):
            mixed[block * ROWS : (block + 1) * ROWS, side * LANES : (side + 1) * LANES] = source[
                row : row + ROWS, col + block * LANES : col + (block + 1) * LANES
            ]
    chunks = dot(pack_ref[...], mixed[...])
    high = chunks.shape[0] // GROUP
    for side in range(2):
        for item in range(GROUP):
            store(
                side,
                item,
                chunks[item * high : (item + 1) * high, side * LANES : (side + 1) * LANES].astype(BF),
            )


def unpack(load, unpack_ref, stage, target, starts):
    high = stage.shape[0] // GROUP
    for side in range(2):
        for item in range(GROUP):
            stage[item * high : (item + 1) * high, side * LANES : (side + 1) * LANES] = load(side, item).astype(F32)
    mixed = dot(unpack_ref[...], stage[...].astype(BF))
    for side, (row, col) in enumerate(starts):
        for block in range(mixed.shape[0] // ROWS):
            target[row : row + ROWS, col + block * LANES : col + (block + 1) * LANES] = mixed[
                block * ROWS : (block + 1) * ROWS, side * LANES : (side + 1) * LANES
            ].astype(BF)


def dispatch_body(count, *refs):
    values, places, weights = refs[:count], refs[count : 2 * count], refs[2 * count : 3 * count]
    pack_ref, out, slots, mixed = refs[3 * count :]
    half = slots.shape[1] // 2
    for index in range(count):
        slots[...] = (dot(places[index][...], values[index][...]) * weights[index][...]).astype(BF)
        for group in range(slots.shape[0] // ROWS):

            def store(side, item, chunk, index=index, group=group):
                out[(group * GROUP + item) * 2 + side, index] = chunk

            pack(slots, [(group * ROWS, 0), (group * ROWS, half)], pack_ref, mixed, store)


def dispatch(values, places, weights, packer, chunk_rows):
    count = len(values)
    slot_count, width = places[0].shape[0], values[0].shape[1]
    experts = slot_count // CAP
    return vmem_call(
        functools.partial(dispatch_body, count),
        jax.ShapeDtypeStruct((2 * experts, count, chunk_rows, LANES), BF),
        [pltpu.VMEM((slot_count, width), BF), pltpu.VMEM((packer.shape[1], 2 * LANES), BF)],
    )(*values, *places, *weights, packer)


def unpack_all(got, index, unpack_ref, stage, rows):
    for pair in range(got.shape[0] // (2 * GROUP)):

        def load(side, item, pair=pair):
            return got[(2 * pair + side) * GROUP + item, index]

        unpack(load, unpack_ref, stage, rows, [(2 * pair * ROWS, 0), ((2 * pair + 1) * ROWS, 0)])


def by_parts(rows, parts, dims, own, sent):
    start = 0
    for part in parts:
        product = dot(rows[...], part[...], dims)
        width = product.shape[1]
        own[:, start : start + width] = product
        sent[:, start : start + width] = product.astype(BF)
        start += width


def arrive_body(index, got, unpack_ref, part0, part1, rows, own, sent, stage):
    unpack_all(got, index, unpack_ref, stage, rows)
    dims = NT if part0.shape[1] == rows.shape[1] else (((1,), (0,)), ((), ()))
    by_parts(rows, (part0, part1), dims, own, sent)


def arrive_either_body(index, flag, got, unpack_ref, up0, up1, down0, down1, rows, own, sent, stage):
    unpack_all(got, index, unpack_ref, stage, rows)

    @pl.when(flag[0] == 1)
    def _():
        by_parts(rows, (down0, down1), NT, own, sent)

    @pl.when(flag[0] == 0)
    def _():
        by_parts(rows, (up0, up1), (((1,), (0,)), ((), ())), own, sent)


def shapes_of(got, hidden, width):
    total = got.shape[0] * CAP
    return (
        jax.ShapeDtypeStruct((total, width), BF),
        jax.ShapeDtypeStruct((total, hidden), F32),
        jax.ShapeDtypeStruct((total, hidden), BF),
    )


def arrive(got, index, unpacker, parts):
    stage = pltpu.VMEM((unpacker.shape[1], 2 * LANES), F32)
    hidden = 2 * min(parts[0].shape)
    return vmem_call(functools.partial(arrive_body, index), shapes_of(got, hidden, max(parts[0].shape)), [stage])(
        got, unpacker, *parts
    )


def arrive_either(flag, got, index, unpacker, ups, downs):
    stage = pltpu.VMEM((unpacker.shape[1], 2 * LANES), F32)
    return vmem_call(
        functools.partial(arrive_either_body, index),
        shapes_of(got, 2 * ups[0].shape[1], ups[0].shape[0]),
        [stage],
        1,
    )(flag, got, unpacker, *ups, *downs)


def turn_body(pre_own, pre_got, act_own, act_got, up0, up1, pack_ref, active, grads, out, rows, mixed):
    pre = pre_own[...] + pre_got[...].astype(F32)
    gate = 1.0 / (1.0 + jnp.exp(-pre))
    active[...] = (pre * gate).astype(BF)
    slope = gate * (1.0 + pre * (1.0 - gate))
    grads[...] = ((act_own[...] + act_got[...].astype(F32)) * slope).astype(BF)
    hidden = up0.shape[1]
    rows[...] = (dot(grads[:, :hidden], up0[...], NT) + dot(grads[:, hidden:], up1[...], NT)).astype(BF)
    for pair in range(out.shape[0] // (2 * GROUP)):

        def store(side, item, chunk, pair=pair):
            out[(2 * pair + side) * GROUP + item, 0] = chunk

        pack(rows, [(2 * pair * ROWS, 0), ((2 * pair + 1) * ROWS, 0)], pack_ref, mixed, store)


def turn(pre_own, pre_got, act_own, act_got, ups, packer, chunk_rows):
    total, hidden = pre_own.shape
    width = ups[0].shape[0]
    kept = jax.ShapeDtypeStruct((total, hidden), BF)
    return vmem_call(
        turn_body,
        (kept, kept, jax.ShapeDtypeStruct((total // CAP, 1, chunk_rows, LANES), BF)),
        [pltpu.VMEM((total, width), BF), pltpu.VMEM((packer.shape[1], 2 * LANES), BF)],
    )(pre_own, pre_got, act_own, act_got, *ups, packer)


def combine_body(got, unpack_ref, place_t, incoming, out, slots, stage):
    half = slots.shape[1] // 2
    for group in range(slots.shape[0] // ROWS):

        def load(side, item, group=group):
            return got[(group * GROUP + item) * 2 + side, 0]

        unpack(load, unpack_ref, stage, slots, [(group * ROWS, 0), (group * ROWS, half)])
    out[...] = (dot(place_t[...], slots[...]) + incoming[...].astype(F32)).astype(BF)


def combine(got, unpacker, place_t, incoming):
    return vmem_call(
        combine_body,
        jax.ShapeDtypeStruct(incoming.shape, BF),
        [
            pltpu.VMEM((place_t.shape[1], incoming.shape[1]), BF),
            pltpu.VMEM((unpacker.shape[1], 2 * LANES), F32),
        ],
    )(got, unpacker, place_t, incoming)


def slots_of(routes, gates, experts):
    tokens, top = routes.shape
    flat = routes.reshape(-1)
    order = jnp.arange(tokens * top, dtype=jnp.int32)
    earlier = (flat[:, None] == flat[None, :]) & (order[None, :] < order[:, None])
    slot = flat * CAP + jnp.sum(earlier.astype(jnp.int32), axis=1)
    hits = slot.reshape(tokens, top)[None] == jnp.arange(experts * CAP, dtype=jnp.int32)[:, None, None]
    place = jnp.any(hits, axis=2)
    weight = jnp.sum(jnp.where(hits, gates[None], 0.0), axis=(1, 2))
    return place.astype(BF), weight[:, None]


def packing(blocks, chunk_rows):
    total = GROUP * chunk_rows
    row = jnp.arange(total, dtype=jnp.int32)
    col = jnp.arange(blocks * ROWS, dtype=jnp.int32)
    item, place = row // chunk_rows, row % chunk_rows
    block, inner = place // CAP, place % CAP
    wanted = jnp.where(block < blocks, block * ROWS + item * CAP + inner, -1)
    return (wanted[:, None] == col[None, :]).astype(BF), (wanted[None, :] == col[:, None]).astype(BF)


def swap(value, axis):
    return lax.ppermute(value, axis, [(0, 1), (1, 0)])


def cross(value):
    moved = lax.ppermute(value, ("dp", "half"), [(1, 2), (2, 1)])
    return jnp.where(lax.axis_index("dp") == lax.axis_index("half"), value, moved)


def send(chunks):
    return lax.all_to_all(chunks, PAIRED, split_axis=0, concat_axis=0, tiled=True)


def on_device(grad_out, layer_in, routes, gates, w_up, w_down):
    section = lax.axis_index("section")
    top_section = section == lax.axis_size("section") - 1
    flag = top_section.astype(jnp.int32)[None]
    experts = lax.axis_size("pair")
    width = grad_out.shape[2]
    blocks = width // (2 * LANES)
    chunk_rows = -(-blocks * CAP // 8) * 8
    packer, unpacker = packing(blocks, chunk_rows)

    place, weight = zip(*[slots_of(routes[0, micro], gates[0, micro], experts) for micro in range(2)])
    place_t = [p.T for p in place]
    ones = jnp.ones_like(weight[0])
    inputs = [layer_in[0, 0], layer_in[0, 1]]

    up_here, down_here = cross(w_up[0, 0]), cross(w_down[0, 0])
    ups = (up_here, swap(up_here, "dp"))
    downs = (down_here, swap(down_here, "dp"))

    def pick(here, there):
        return jnp.where(top_section, here, there)

    def prepare(values, places, weights):
        return dispatch(values, places, weights, packer, chunk_rows)

    def top_start():
        first = send(prepare([inputs[0], grad_out[0]], [place[0]] * 2, [ones, weight[0]]))
        return first, prepare([inputs[1], grad_out[1]], [place[1]] * 2, [ones, weight[1]])

    def low_start():
        chunks = prepare(inputs, place, [ones, ones])
        return jnp.zeros_like(chunks), chunks

    first, second_chunks = lax.cond(top_section, top_start, low_start)
    first, second_chunks, unpacker = lax.optimization_barrier((first, second_chunks, unpacker))
    second = send(second_chunks)

    rows_a0, own_a0, sent_a0 = arrive(first, 0, unpacker, ups)
    got_a0 = swap(sent_a0, "half")
    rows_a1, own_a1, sent_a1 = arrive(first, 1, unpacker, downs)
    got_a1 = swap(sent_a1, "half")
    top_active0, top_grads0, back0 = turn(own_a0, got_a0, own_a1, got_a1, ups, packer, chunk_rows)
    second, back0 = lax.optimization_barrier((second, back0))
    third = send(back0)

    rows_b0, own_b0, sent_b0 = arrive(second, 0, unpacker, ups)
    got_b0 = swap(sent_b0, "half")
    rows_b1, own_b1, sent_b1 = arrive_either(flag, second, 1, unpacker, ups, downs)
    got_b1 = swap(sent_b1, "half")
    top_active1, top_grads1, back1 = turn(own_b0, got_b0, own_b1, got_b1, ups, packer, chunk_rows)

    top_out0 = combine(third, unpacker, place_t[0], grad_out[0])
    low_in0 = lax.ppermute(top_out0, "section", [(1, 0)])
    fourth_chunks = pick(back1, dispatch([low_in0], [place[0]], [weight[0]], packer, chunk_rows))
    rows_in0, rows_in1 = pick(rows_a0, rows_b0), pick(rows_b0, rows_b1)
    fourth = send(fourth_chunks)
    top_out1 = combine(fourth, unpacker, place_t[1], grad_out[1])
    low_in1 = lax.ppermute(top_out1, "section", [(1, 0)])
    rows_d, own_d, sent_d = arrive(fourth, 0, unpacker, downs)
    low_in1, sent_d = lax.optimization_barrier((low_in1, sent_d))
    got_d = swap(sent_d, "half")

    fifth = send(dispatch([low_in1], [place[1]], [weight[1]], packer, chunk_rows))
    low_active0, low_grads0, back2 = turn(own_b0, got_b0, own_d, got_d, ups, packer, chunk_rows)
    fifth, back2 = lax.optimization_barrier((fifth, back2))
    sixth = send(back2)
    rows_e, own_e, sent_e = arrive(fifth, 0, unpacker, downs)
    got_e = swap(sent_e, "half")
    low_active1, low_grads1, back3 = turn(own_b1, got_b1, own_e, got_e, ups, packer, chunk_rows)
    seventh = send(back3)

    def both(top0, top1, low0, low1):
        return jnp.concatenate([pick(top0, low0), pick(top1, low1)])

    hidden = own_a0.shape[1] // 2
    over = (((0,), (0,)), ((), ()))
    rows = jnp.concatenate([rows_in0, rows_in1])
    scaled = both(rows_a1, rows_b1, rows_d, rows_e)
    sixth, low_active1, low_grads1, scaled, rows = lax.optimization_barrier(
        (sixth, low_active1, low_grads1, scaled, rows)
    )
    active = both(top_active0, top_active1, low_active0, low_active1)
    grads = both(top_grads0, top_grads1, low_grads0, low_grads1)
    other_up = swap(dot(rows, grads[:, hidden:], over).astype(BF), "dp")
    other_down = swap(dot(active[:, hidden:], scaled, over).astype(BF), "dp")
    grad_up = (dot(rows, grads[:, :hidden], over) + other_up.astype(F32)).astype(BF)
    grad_down = (dot(active[:, :hidden], scaled, over) + other_down.astype(F32)).astype(BF)
    grad_up, grad_down = cross(grad_up), cross(grad_down)
    seventh, grad_up, grad_down = lax.optimization_barrier((seventh, grad_up, grad_down))
    low_out0 = combine(sixth, unpacker, place_t[0], low_in0)
    low_out1 = combine(seventh, unpacker, place_t[1], low_in1)
    results = jnp.stack([pick(top_out0, low_out0), pick(top_out1, low_out1)])
    return results[None], grad_up[None, None], grad_down[None, None]


def solution(mesh):
    sizes = dict(zip(mesh.axis_names, mesh.devices.shape))
    fine = Mesh(
        mesh.devices.reshape(sizes["section"], sizes["dp"], sizes["expert"] // 2, 2),
        ("section", "dp", "pair", "half"),
    )
    tokens = P("section", None, ("dp", "pair", "half"), None)
    up, down = P("section", PAIRED, "dp", None), P("section", PAIRED, None, "dp")
    return jax.shard_map(
        on_device,
        mesh=fine,
        in_specs=(P(None, ("dp", "pair", "half"), None), tokens, tokens, tokens, up, down),
        out_specs=(tokens, up, down),
        check_vma=False,
    )
```

```python
import functools

import jax
import jax.numpy as jnp
from jax import lax
from jax.experimental import pallas as pl
from jax.experimental.pallas import tpu as pltpu
from jax.sharding import Mesh, PartitionSpec as P

BF = jnp.bfloat16
F32 = jnp.float32
LANES = 128
GROUP = 16
VMEM_BYTES = 56 << 20
CAP = 5
PAIRED = ("pair", "half")
ROWS = GROUP * CAP
NT = (((1,), (1,)), ((), ()))


def staged_call(body, inputs, small, outs, scratch=()):
    outs_flat = [outs] if isinstance(outs, jax.ShapeDtypeStruct) else list(outs)
    n_in, n_small, n_out = len(inputs), len(small), len(outs_flat)
    held = []
    for array, index in inputs:
        shape = tuple(size for size, at in zip(array.shape, index) if isinstance(at, slice)) + array.shape[len(index) :]
        held.append(pltpu.VMEM(shape, array.dtype))

    def kernel(*refs):
        sources, refs = refs[:n_in], refs[n_in:]
        little, refs = refs[:n_small], refs[n_small:]
        targets, refs = refs[:n_out], refs[n_out:]
        taken, refs = refs[:n_in], refs[n_in:]
        made, refs = refs[:n_out], refs[n_out:]
        in_sems, out_sems, rest = refs[0], refs[1], refs[2:]
        loads = [
            pltpu.make_async_copy(ref.at[index] if index else ref, here, in_sems.at[i])
            for i, (ref, (_, index), here) in enumerate(zip(sources, inputs, taken))
        ]
        stores = [pltpu.make_async_copy(here, ref, out_sems.at[i]) for i, (here, ref) in enumerate(zip(made, targets))]
        for load in loads:
            load.start()
        body(taken, lambda i: loads[i].wait(), little, made, lambda i: stores[i].start(), rest)
        for store in stores:
            store.wait()

    anywhere, vmem = pl.BlockSpec(memory_space=pl.ANY), pl.BlockSpec(memory_space=pltpu.VMEM)
    result = pl.pallas_call(
        kernel,
        out_shape=outs_flat,
        in_specs=[anywhere] * n_in + [vmem] * n_small,
        out_specs=[anywhere] * n_out,
        scratch_shapes=held
        + [pltpu.VMEM(out.shape, out.dtype) for out in outs_flat]
        + [pltpu.SemaphoreType.DMA((n_in,)), pltpu.SemaphoreType.DMA((n_out,))]
        + list(scratch),
        cost_estimate=pl.CostEstimate(flops=1, bytes_accessed=1, transcendentals=0),
        compiler_params=pltpu.CompilerParams(vmem_limit_bytes=VMEM_BYTES),
    )(*[array for array, _ in inputs], *small)
    return result[0] if isinstance(outs, jax.ShapeDtypeStruct) else tuple(result)


def dot(a, b, dims=(((1,), (0,)), ((), ()))):
    return lax.dot_general(a, b, dims, preferred_element_type=F32)


def pack(source, starts, pack_ref, mixed, store):
    blocks = mixed.shape[0] // ROWS
    for side, (row, col) in enumerate(starts):
        for block in range(blocks):
            mixed[block * ROWS : (block + 1) * ROWS, side * LANES : (side + 1) * LANES] = source[
                row : row + ROWS, col + block * LANES : col + (block + 1) * LANES
            ]
    chunks = dot(pack_ref[...], mixed[...])
    high = chunks.shape[0] // GROUP
    for side in range(2):
        for item in range(GROUP):
            store(
                side,
                item,
                chunks[item * high : (item + 1) * high, side * LANES : (side + 1) * LANES].astype(BF),
            )


def unpack(load, unpack_ref, stage, target, starts):
    high = stage.shape[0] // GROUP
    for side in range(2):
        for item in range(GROUP):
            stage[item * high : (item + 1) * high, side * LANES : (side + 1) * LANES] = load(side, item).astype(F32)
    mixed = dot(unpack_ref[...], stage[...].astype(BF))
    for side, (row, col) in enumerate(starts):
        for block in range(mixed.shape[0] // ROWS):
            target[row : row + ROWS, col + block * LANES : col + (block + 1) * LANES] = mixed[
                block * ROWS : (block + 1) * ROWS, side * LANES : (side + 1) * LANES
            ].astype(BF)


def dispatch(values, places, weights, packer, chunk_rows):
    count, width = len(values), values[0][0].shape[-1]
    slot_count = places[0].shape[0]

    def body(taken, wait, little, made, put, scratch):
        slots, mixed = scratch
        pack_ref, out = taken[count], made[0]
        for index in range(count):
            wait(index)
            place, weight = little[index], little[count + index]
            slots[...] = (dot(place[...], taken[index][...]) * weight[...]).astype(BF)
            if index == 0:
                wait(count)
            for group in range(slot_count // ROWS):

                def store(side, item, chunk, index=index, group=group):
                    out[(group * GROUP + item) * 2 + side, index] = chunk

                pack(slots, [(group * ROWS, 0), (group * ROWS, width // 2)], pack_ref, mixed, store)
        put(0)

    return staged_call(
        body,
        [*values, (packer, ())],
        [*places, *weights],
        jax.ShapeDtypeStruct((2 * slot_count // CAP, count, chunk_rows, LANES), BF),
        [pltpu.VMEM((slot_count, width), BF), pltpu.VMEM((packer.shape[1], 2 * LANES), BF)],
    )


def arrive(got, index, unpacker, parts):
    hidden, width, total = 2 * min(parts[0].shape), max(parts[0].shape), got.shape[0] * CAP
    dims = NT if parts[0].shape[1] == width else (((1,), (0,)), ((), ()))

    def body(taken, wait, little, made, put, scratch):
        chunks, unpack_ref, *weights = taken
        rows, own, sent = made
        wait(0)
        wait(1)
        for pair in range(chunks.shape[0] // (2 * GROUP)):

            def load(side, item, pair=pair):
                return chunks[(2 * pair + side) * GROUP + item]

            unpack(load, unpack_ref, scratch[0], rows, [(2 * pair * ROWS, 0), ((2 * pair + 1) * ROWS, 0)])
        put(0)
        for number, part in enumerate(weights):
            wait(2 + number)
            product = dot(rows[...], part[...], dims)
            columns = slice(number * hidden // 2, (number + 1) * hidden // 2)
            own[:, columns] = product
            sent[:, columns] = product.astype(BF)
        put(2)
        put(1)

    return staged_call(
        body,
        [(got, (slice(None), index)), (unpacker, ()), (parts[0], ()), (parts[1], ())],
        [],
        (
            jax.ShapeDtypeStruct((total, width), BF),
            jax.ShapeDtypeStruct((total, hidden), F32),
            jax.ShapeDtypeStruct((total, hidden), BF),
        ),
        [pltpu.VMEM((unpacker.shape[1], 2 * LANES), F32)],
    )


def turn(pre_own, pre_got, act_own, act_got, ups, packer, chunk_rows):
    total, hidden = pre_own.shape
    width = ups[0].shape[0]

    def body(taken, wait, little, made, put, scratch):
        pre_here, pre_there, act_here, act_there, up0, up1, pack_ref = taken
        active, grads, out = made
        rows, mixed = scratch
        wait(0)
        wait(1)
        pre = pre_here[...] + pre_there[...].astype(F32)
        gate = 1.0 / (1.0 + jnp.exp(-pre))
        active[...] = (pre * gate).astype(BF)
        put(0)
        slope = gate * (1.0 + pre * (1.0 - gate))
        wait(2)
        wait(3)
        grads[...] = ((act_here[...] + act_there[...].astype(F32)) * slope).astype(BF)
        put(1)
        wait(4)
        wait(5)
        rows[...] = (dot(grads[:, : hidden // 2], up0[...], NT) + dot(grads[:, hidden // 2 :], up1[...], NT)).astype(BF)
        wait(6)
        for pair in range(out.shape[0] // (2 * GROUP)):

            def store(side, item, chunk, pair=pair):
                out[(2 * pair + side) * GROUP + item, 0] = chunk

            pack(rows, [(2 * pair * ROWS, 0), ((2 * pair + 1) * ROWS, 0)], pack_ref, mixed, store)
        put(2)

    kept = jax.ShapeDtypeStruct((total, hidden), BF)
    return staged_call(
        body,
        [(array, ()) for array in (pre_own, pre_got, act_own, act_got, *ups, packer)],
        [],
        (kept, kept, jax.ShapeDtypeStruct((total // CAP, 1, chunk_rows, LANES), BF)),
        [pltpu.VMEM((total, width), BF), pltpu.VMEM((packer.shape[1], 2 * LANES), BF)],
    )


def combine(got, unpacker, place_t, incoming):
    array, index = incoming
    tokens, width = array.shape[-2:]

    def body(taken, wait, little, made, put, scratch):
        chunks, unpack_ref, base = taken
        slots, stage = scratch
        wait(0)
        wait(1)
        for group in range(slots.shape[0] // ROWS):

            def load(side, item, group=group):
                return chunks[(group * GROUP + item) * 2 + side]

            unpack(load, unpack_ref, stage, slots, [(group * ROWS, 0), (group * ROWS, width // 2)])
        wait(2)
        made[0][...] = (dot(little[0][...], slots[...]) + base[...].astype(F32)).astype(BF)
        put(0)

    return staged_call(
        body,
        [(got, (slice(None), 0)), (unpacker, ()), incoming],
        [place_t],
        jax.ShapeDtypeStruct((tokens, width), BF),
        [pltpu.VMEM((place_t.shape[1], width), BF), pltpu.VMEM((unpacker.shape[1], 2 * LANES), F32)],
    )


def slots_of(routes, gates, experts):
    tokens, top = routes.shape
    flat = routes.reshape(-1)
    order = jnp.arange(tokens * top, dtype=jnp.int32)
    earlier = (flat[:, None] == flat[None, :]) & (order[None, :] < order[:, None])
    slot = flat * CAP + jnp.sum(earlier.astype(jnp.int32), axis=1)
    hits = slot.reshape(tokens, top)[None] == jnp.arange(experts * CAP, dtype=jnp.int32)[:, None, None]
    place = jnp.any(hits, axis=2)
    weight = jnp.sum(jnp.where(hits, gates[None], 0.0), axis=(1, 2))
    return place.astype(BF), weight[:, None]


def packing(blocks, chunk_rows):
    total = GROUP * chunk_rows
    row = jnp.arange(total, dtype=jnp.int32)
    col = jnp.arange(blocks * ROWS, dtype=jnp.int32)
    item, place = row // chunk_rows, row % chunk_rows
    block, inner = place // CAP, place % CAP
    wanted = jnp.where(block < blocks, block * ROWS + item * CAP + inner, -1)
    return (wanted[:, None] == col[None, :]).astype(BF), (wanted[None, :] == col[:, None]).astype(BF)


def swap(value, axis):
    return lax.ppermute(value, axis, [(0, 1), (1, 0)])


def cross(value):
    moved = lax.ppermute(value, ("dp", "half"), [(1, 2), (2, 1)])
    return jnp.where(lax.axis_index("dp") == lax.axis_index("half"), value, moved)


def send(chunks):
    return lax.all_to_all(chunks, PAIRED, split_axis=0, concat_axis=0, tiled=True)


def on_device(grad_out, layer_in, routes, gates, w_up, w_down):
    section = lax.axis_index("section")
    top_section = section == lax.axis_size("section") - 1
    experts = lax.axis_size("pair")
    width = grad_out.shape[2]
    blocks = width // (2 * LANES)
    chunk_rows = -(-blocks * CAP // 8) * 8
    packer, unpacker = packing(blocks, chunk_rows)

    place, weight = zip(*[slots_of(routes[0, micro], gates[0, micro], experts) for micro in range(2)])
    place_t = [p.T for p in place]
    ones = jnp.ones_like(weight[0])
    inputs = [(layer_in, (0, 0)), (layer_in, (0, 1))]
    outer = [(grad_out, (0,)), (grad_out, (1,))]

    up_here, down_here = cross(w_up[0, 0]), cross(w_down[0, 0])
    ups = (up_here, swap(up_here, "dp"))
    downs = (down_here, swap(down_here, "dp"))

    def pick(here, there):
        return jnp.where(top_section, here, there)

    def prepare(values, places, weights):
        return dispatch(values, places, weights, packer, chunk_rows)

    def top_start():
        first = send(prepare([inputs[0], outer[0]], [place[0]] * 2, [ones, weight[0]]))
        return first, prepare([inputs[1], outer[1]], [place[1]] * 2, [ones, weight[1]])

    def low_start():
        chunks = prepare(inputs, place, [ones, ones])
        return jnp.zeros_like(chunks), chunks

    first, second_chunks = lax.cond(top_section, top_start, low_start)
    first, second_chunks, unpacker = lax.optimization_barrier((first, second_chunks, unpacker))
    second = send(second_chunks)

    rows_a0, own_a0, sent_a0 = arrive(first, 0, unpacker, ups)
    got_a0 = swap(sent_a0, "half")
    rows_a1, own_a1, sent_a1 = arrive(first, 1, unpacker, downs)
    got_a1 = swap(sent_a1, "half")
    top_active0, top_grads0, back0 = turn(own_a0, got_a0, own_a1, got_a1, ups, packer, chunk_rows)
    second, back0 = lax.optimization_barrier((second, back0))
    third = send(back0)

    rows_b0, own_b0, sent_b0 = arrive(second, 0, unpacker, ups)
    got_b0 = swap(sent_b0, "half")
    rows_b1, own_b1, sent_b1 = lax.cond(
        top_section, lambda: arrive(second, 1, unpacker, downs), lambda: arrive(second, 1, unpacker, ups)
    )
    got_b1 = swap(sent_b1, "half")
    top_active1, top_grads1, back1 = turn(own_b0, got_b0, own_b1, got_b1, ups, packer, chunk_rows)

    top_out0 = combine(third, unpacker, place_t[0], outer[0])
    low_in0 = lax.ppermute(top_out0, "section", [(1, 0)])
    fourth_chunks = pick(back1, dispatch([(low_in0, ())], [place[0]], [weight[0]], packer, chunk_rows))
    rows_in0, rows_in1 = pick(rows_a0, rows_b0), pick(rows_b0, rows_b1)
    fourth = send(fourth_chunks)
    top_out1 = combine(fourth, unpacker, place_t[1], outer[1])
    low_in1 = lax.ppermute(top_out1, "section", [(1, 0)])
    rows_d, own_d, sent_d = arrive(fourth, 0, unpacker, downs)
    low_in1, sent_d = lax.optimization_barrier((low_in1, sent_d))
    got_d = swap(sent_d, "half")

    fifth = send(dispatch([(low_in1, ())], [place[1]], [weight[1]], packer, chunk_rows))
    low_active0, low_grads0, back2 = turn(own_b0, got_b0, own_d, got_d, ups, packer, chunk_rows)
    fifth, back2 = lax.optimization_barrier((fifth, back2))
    sixth = send(back2)
    rows_e, own_e, sent_e = arrive(fifth, 0, unpacker, downs)
    got_e = swap(sent_e, "half")
    low_active1, low_grads1, back3 = turn(own_b1, got_b1, own_e, got_e, ups, packer, chunk_rows)
    seventh = send(back3)

    def both(top0, top1, low0, low1):
        return jnp.concatenate([pick(top0, low0), pick(top1, low1)])

    hidden = own_a0.shape[1] // 2
    over = (((0,), (0,)), ((), ()))
    rows = jnp.concatenate([rows_in0, rows_in1])
    scaled = both(rows_a1, rows_b1, rows_d, rows_e)
    sixth, low_active1, low_grads1, scaled, rows = lax.optimization_barrier(
        (sixth, low_active1, low_grads1, scaled, rows)
    )
    active = both(top_active0, top_active1, low_active0, low_active1)
    grads = both(top_grads0, top_grads1, low_grads0, low_grads1)
    other_up = swap(dot(rows, grads[:, hidden:], over).astype(BF), "dp")
    other_down = swap(dot(active[:, hidden:], scaled, over).astype(BF), "dp")
    grad_up = (dot(rows, grads[:, :hidden], over) + other_up.astype(F32)).astype(BF)
    grad_down = (dot(active[:, :hidden], scaled, over) + other_down.astype(F32)).astype(BF)
    grad_up, grad_down = cross(grad_up), cross(grad_down)
    seventh, grad_up, grad_down = lax.optimization_barrier((seventh, grad_up, grad_down))
    low_out0 = combine(sixth, unpacker, place_t[0], (low_in0, ()))
    low_out1 = combine(seventh, unpacker, place_t[1], (low_in1, ()))
    results = jnp.stack([pick(top_out0, low_out0), pick(top_out1, low_out1)])
    return results[None], grad_up[None, None], grad_down[None, None]


def solution(mesh):
    sizes = dict(zip(mesh.axis_names, mesh.devices.shape))
    fine = Mesh(
        mesh.devices.reshape(sizes["section"], sizes["dp"], sizes["expert"] // 2, 2),
        ("section", "dp", "pair", "half"),
    )
    tokens = P("section", None, ("dp", "pair", "half"), None)
    up, down = P("section", PAIRED, "dp", None), P("section", PAIRED, None, "dp")
    return jax.shard_map(
        on_device,
        mesh=fine,
        in_specs=(P(None, ("dp", "pair", "half"), None), tokens, tokens, tokens, up, down),
        out_specs=(tokens, up, down),
        check_vma=False,
    )
```

```python
import functools

import jax
import jax.numpy as jnp
from jax import lax
from jax.experimental import pallas as pl
from jax.experimental.pallas import tpu as pltpu
from jax.sharding import Mesh, PartitionSpec as P

BF = jnp.bfloat16
F32 = jnp.float32
LANES = 128
GROUP = 16
VMEM_BYTES = 56 << 20
CAP = 5
PAIRED = ("pair", "half")
ROWS = GROUP * CAP
NT = (((1,), (1,)), ((), ()))


def staged_call(body, inputs, small, outs, scratch=()):
    outs_flat = [outs] if isinstance(outs, jax.ShapeDtypeStruct) else list(outs)
    n_in, n_small, n_out = len(inputs), len(small), len(outs_flat)
    held = []
    for array, index in inputs:
        shape = tuple(size for size, at in zip(array.shape, index) if isinstance(at, slice)) + array.shape[len(index) :]
        held.append(pltpu.VMEM(shape, array.dtype))

    def kernel(*refs):
        sources, refs = refs[:n_in], refs[n_in:]
        little, refs = refs[:n_small], refs[n_small:]
        targets, refs = refs[:n_out], refs[n_out:]
        taken, refs = refs[:n_in], refs[n_in:]
        made, refs = refs[:n_out], refs[n_out:]
        in_sems, out_sems, rest = refs[0], refs[1], refs[2:]
        loads = [
            pltpu.make_async_copy(ref.at[index] if index else ref, here, in_sems.at[i])
            for i, (ref, (_, index), here) in enumerate(zip(sources, inputs, taken))
        ]
        stores = [pltpu.make_async_copy(here, ref, out_sems.at[i]) for i, (here, ref) in enumerate(zip(made, targets))]
        for load in loads:
            load.start()
        body(taken, lambda i: loads[i].wait(), little, made, lambda i: stores[i].start(), rest)
        for store in stores:
            store.wait()

    anywhere, vmem = pl.BlockSpec(memory_space=pl.ANY), pl.BlockSpec(memory_space=pltpu.VMEM)
    result = pl.pallas_call(
        kernel,
        out_shape=outs_flat,
        in_specs=[anywhere] * n_in + [vmem] * n_small,
        out_specs=[anywhere] * n_out,
        scratch_shapes=held
        + [pltpu.VMEM(out.shape, out.dtype) for out in outs_flat]
        + [pltpu.SemaphoreType.DMA((n_in,)), pltpu.SemaphoreType.DMA((n_out,))]
        + list(scratch),
        cost_estimate=pl.CostEstimate(flops=1, bytes_accessed=1, transcendentals=0),
        compiler_params=pltpu.CompilerParams(vmem_limit_bytes=VMEM_BYTES),
    )(*[array for array, _ in inputs], *small)
    return result[0] if isinstance(outs, jax.ShapeDtypeStruct) else tuple(result)


def dot(a, b, dims=(((1,), (0,)), ((), ()))):
    return lax.dot_general(a, b, dims, preferred_element_type=F32)


def pack(source, starts, pack_ref, mixed, store):
    blocks = mixed.shape[0] // ROWS
    for side, (row, col) in enumerate(starts):
        for block in range(blocks):
            mixed[block * ROWS : (block + 1) * ROWS, side * LANES : (side + 1) * LANES] = source[
                row : row + ROWS, col + block * LANES : col + (block + 1) * LANES
            ]
    chunks = dot(pack_ref[...], mixed[...])
    high = chunks.shape[0] // GROUP
    for side in range(2):
        for item in range(GROUP):
            store(
                side,
                item,
                chunks[item * high : (item + 1) * high, side * LANES : (side + 1) * LANES].astype(BF),
            )


def unpack(load, unpack_ref, stage, target, starts):
    high = stage.shape[0] // GROUP
    for side in range(2):
        for item in range(GROUP):
            stage[item * high : (item + 1) * high, side * LANES : (side + 1) * LANES] = load(side, item).astype(F32)
    mixed = dot(unpack_ref[...], stage[...].astype(BF))
    for side, (row, col) in enumerate(starts):
        for block in range(mixed.shape[0] // ROWS):
            target[row : row + ROWS, col + block * LANES : col + (block + 1) * LANES] = mixed[
                block * ROWS : (block + 1) * ROWS, side * LANES : (side + 1) * LANES
            ].astype(BF)


def dispatch(values, places, weights, packer, chunk_rows):
    count, width = len(values), values[0][0].shape[-1]
    slot_count = places[0].shape[0]

    def body(taken, wait, little, made, put, scratch):
        slots, mixed = scratch
        pack_ref, out = taken[count], made[0]
        for index in range(count):
            wait(index)
            place, weight = little[index], little[count + index]
            slots[...] = (dot(place[...], taken[index][...]) * weight[...]).astype(BF)
            if index == 0:
                wait(count)
            for group in range(slot_count // ROWS):

                def store(side, item, chunk, index=index, group=group):
                    out[(group * GROUP + item) * 2 + side, index] = chunk

                pack(slots, [(group * ROWS, 0), (group * ROWS, width // 2)], pack_ref, mixed, store)
        put(0)

    return staged_call(
        body,
        [*values, (packer, ())],
        [*places, *weights],
        jax.ShapeDtypeStruct((2 * slot_count // CAP, count, chunk_rows, LANES), BF),
        [pltpu.VMEM((slot_count, width), BF), pltpu.VMEM((packer.shape[1], 2 * LANES), BF)],
    )


def arrive(got, index, unpacker, parts):
    hidden, width, total = 2 * min(parts[0].shape), max(parts[0].shape), got.shape[0] * CAP
    dims = NT if parts[0].shape[1] == width else (((1,), (0,)), ((), ()))

    def body(taken, wait, little, made, put, scratch):
        chunks, unpack_ref, *weights = taken
        rows, own, sent = made
        wait(0)
        wait(1)
        for pair in range(chunks.shape[0] // (2 * GROUP)):

            def load(side, item, pair=pair):
                return chunks[(2 * pair + side) * GROUP + item]

            unpack(load, unpack_ref, scratch[0], rows, [(2 * pair * ROWS, 0), ((2 * pair + 1) * ROWS, 0)])
        put(0)
        for number, part in enumerate(weights):
            wait(2 + number)
            product = dot(rows[...], part[...], dims)
            columns = slice(number * hidden // 2, (number + 1) * hidden // 2)
            own[:, columns] = product
            sent[:, columns] = product.astype(BF)
        put(2)
        put(1)

    return staged_call(
        body,
        [(got, (slice(None), index)), (unpacker, ()), (parts[0], ()), (parts[1], ())],
        [],
        (
            jax.ShapeDtypeStruct((total, width), BF),
            jax.ShapeDtypeStruct((total, hidden), F32),
            jax.ShapeDtypeStruct((total, hidden), BF),
        ),
        [pltpu.VMEM((unpacker.shape[1], 2 * LANES), F32)],
    )


def turn(pre_own, pre_got, act_own, act_got, ups, packer, chunk_rows):
    total, hidden = pre_own.shape
    width = ups[0].shape[0]

    def body(taken, wait, little, made, put, scratch):
        pre_here, pre_there, act_here, act_there, up0, up1, pack_ref = taken
        active, grads, out = made
        rows, mixed = scratch
        wait(0)
        wait(1)
        pre = pre_here[...] + pre_there[...].astype(F32)
        gate = 1.0 / (1.0 + jnp.exp(-pre))
        active[...] = (pre * gate).astype(BF)
        put(0)
        slope = gate * (1.0 + pre * (1.0 - gate))
        wait(2)
        wait(3)
        grads[...] = ((act_here[...] + act_there[...].astype(F32)) * slope).astype(BF)
        put(1)
        wait(4)
        wait(5)
        rows[...] = (dot(grads[:, : hidden // 2], up0[...], NT) + dot(grads[:, hidden // 2 :], up1[...], NT)).astype(BF)
        wait(6)
        for pair in range(out.shape[0] // (2 * GROUP)):

            def store(side, item, chunk, pair=pair):
                out[(2 * pair + side) * GROUP + item, 0] = chunk

            pack(rows, [(2 * pair * ROWS, 0), ((2 * pair + 1) * ROWS, 0)], pack_ref, mixed, store)
        put(2)

    kept = jax.ShapeDtypeStruct((total, hidden), BF)
    return staged_call(
        body,
        [(array, ()) for array in (pre_own, pre_got, act_own, act_got, *ups, packer)],
        [],
        (kept, kept, jax.ShapeDtypeStruct((total // CAP, 1, chunk_rows, LANES), BF)),
        [pltpu.VMEM((total, width), BF), pltpu.VMEM((packer.shape[1], 2 * LANES), BF)],
    )


def combine(got, unpacker, place_t, incoming):
    array, index = incoming
    tokens, width = array.shape[-2:]

    def body(taken, wait, little, made, put, scratch):
        chunks, unpack_ref, base = taken
        slots, stage = scratch
        wait(0)
        wait(1)
        for group in range(slots.shape[0] // ROWS):

            def load(side, item, group=group):
                return chunks[(group * GROUP + item) * 2 + side]

            unpack(load, unpack_ref, stage, slots, [(group * ROWS, 0), (group * ROWS, width // 2)])
        wait(2)
        made[0][...] = (dot(little[0][...], slots[...]) + base[...].astype(F32)).astype(BF)
        put(0)

    return staged_call(
        body,
        [(got, (slice(None), 0)), (unpacker, ()), incoming],
        [place_t],
        jax.ShapeDtypeStruct((tokens, width), BF),
        [pltpu.VMEM((place_t.shape[1], width), BF), pltpu.VMEM((unpacker.shape[1], 2 * LANES), F32)],
    )


def slots_of(routes, gates, experts):
    tokens, top = routes.shape
    flat = routes.reshape(-1)
    order = jnp.arange(tokens * top, dtype=jnp.int32)
    earlier = (flat[:, None] == flat[None, :]) & (order[None, :] < order[:, None])
    slot = flat * CAP + jnp.sum(earlier.astype(jnp.int32), axis=1)
    hits = slot.reshape(tokens, top)[None] == jnp.arange(experts * CAP, dtype=jnp.int32)[:, None, None]
    place = jnp.any(hits, axis=2)
    weight = jnp.sum(jnp.where(hits, gates[None], 0.0), axis=(1, 2))
    return place.astype(BF), weight[:, None]


def packing(blocks, chunk_rows):
    total = GROUP * chunk_rows
    row = jnp.arange(total, dtype=jnp.int32)
    col = jnp.arange(blocks * ROWS, dtype=jnp.int32)
    item, place = row // chunk_rows, row % chunk_rows
    block, inner = place // CAP, place % CAP
    wanted = jnp.where(block < blocks, block * ROWS + item * CAP + inner, -1)
    return (wanted[:, None] == col[None, :]).astype(BF), (wanted[None, :] == col[:, None]).astype(BF)


def swap(value, axis):
    return lax.ppermute(value, axis, [(0, 1), (1, 0)])


def cross(value):
    moved = lax.ppermute(value, ("dp", "half"), [(1, 2), (2, 1)])
    return jnp.where(lax.axis_index("dp") == lax.axis_index("half"), value, moved)


def send(chunks):
    return lax.all_to_all(chunks, PAIRED, split_axis=0, concat_axis=0, tiled=True)


def on_device(grad_out, layer_in, routes, gates, w_up, w_down):
    section = lax.axis_index("section")
    top_section = section == lax.axis_size("section") - 1
    experts = lax.axis_size("pair")
    width = grad_out.shape[2]
    blocks = width // (2 * LANES)
    chunk_rows = -(-blocks * CAP // 8) * 8
    packer, unpacker = packing(blocks, chunk_rows)

    place, weight = zip(*[slots_of(routes[0, micro], gates[0, micro], experts) for micro in range(2)])
    place_t = [p.T for p in place]
    ones = jnp.ones_like(weight[0])
    inputs = [(layer_in, (0, 0)), (layer_in, (0, 1))]
    outer = [(grad_out, (0,)), (grad_out, (1,))]

    up_here, down_here = cross(w_up[0, 0]), cross(w_down[0, 0])
    ups = (up_here, swap(up_here, "dp"))
    downs = (down_here, swap(down_here, "dp"))

    def pick(here, there):
        return jnp.where(top_section, here, there)

    def prepare(values, places, weights):
        return dispatch(values, places, weights, packer, chunk_rows)

    def top_start():
        first = send(prepare([inputs[0], outer[0]], [place[0]] * 2, [ones, weight[0]]))
        return first, prepare([inputs[1], outer[1]], [place[1]] * 2, [ones, weight[1]])

    def low_start():
        chunks = prepare(inputs, place, [ones, ones])
        return jnp.zeros_like(chunks), chunks

    first, second_chunks = lax.cond(top_section, top_start, low_start)
    first, second_chunks, unpacker = lax.optimization_barrier((first, second_chunks, unpacker))
    second = send(second_chunks)

    rows_a0, own_a0, sent_a0 = arrive(first, 0, unpacker, ups)
    got_a0 = swap(sent_a0, "half")
    rows_a1, own_a1, sent_a1 = arrive(first, 1, unpacker, downs)
    got_a1 = swap(sent_a1, "half")
    top_active0, top_grads0, back0 = turn(own_a0, got_a0, own_a1, got_a1, ups, packer, chunk_rows)
    second, back0 = lax.optimization_barrier((second, back0))
    third = send(back0)

    rows_b0, own_b0, sent_b0 = arrive(second, 0, unpacker, ups)
    got_b0 = swap(sent_b0, "half")
    rows_b1, own_b1, sent_b1 = lax.cond(
        top_section, lambda: arrive(second, 1, unpacker, downs), lambda: arrive(second, 1, unpacker, ups)
    )
    got_b1 = swap(sent_b1, "half")
    top_out0 = combine(third, unpacker, place_t[0], outer[0])
    low_in0 = lax.ppermute(top_out0, "section", [(1, 0)])

    def top_turn():
        return turn(own_b0, got_b0, own_b1, got_b1, ups, packer, chunk_rows)

    def low_send():
        kept = jnp.zeros(own_b0.shape, BF)
        return kept, kept, dispatch([(low_in0, ())], [place[0]], [weight[0]], packer, chunk_rows)

    top_active1, top_grads1, fourth_chunks = lax.cond(top_section, top_turn, low_send)
    rows_in0, rows_in1 = pick(rows_a0, rows_b0), pick(rows_b0, rows_b1)
    fourth = send(fourth_chunks)

    def top_combine():
        return combine(fourth, unpacker, place_t[1], outer[1]), rows_b1, own_b1, sent_b1

    def low_arrive():
        return low_in0, *arrive(fourth, 0, unpacker, downs)

    top_out1, rows_d, own_d, sent_d = lax.cond(top_section, top_combine, low_arrive)
    low_in1 = lax.ppermute(top_out1, "section", [(1, 0)])
    got_d = swap(sent_d, "half")

    fifth = send(dispatch([(low_in1, ())], [place[1]], [weight[1]], packer, chunk_rows))
    low_active0, low_grads0, back2 = turn(own_b0, got_b0, own_d, got_d, ups, packer, chunk_rows)
    fifth, back2 = lax.optimization_barrier((fifth, back2))
    rows_e, own_e, sent_e = arrive(fifth, 0, unpacker, downs)
    sent_e, back2 = lax.optimization_barrier((sent_e, back2))
    got_e = swap(sent_e, "half")
    sixth = send(back2)
    low_active1, low_grads1, back3 = turn(own_b1, got_b1, own_e, got_e, ups, packer, chunk_rows)
    seventh = send(back3)

    def both(top0, top1, low0, low1):
        return jnp.concatenate([pick(top0, low0), pick(top1, low1)])

    hidden = own_a0.shape[1] // 2
    over = (((0,), (0,)), ((), ()))
    rows = jnp.concatenate([rows_in0, rows_in1])
    scaled = both(rows_a1, rows_b1, rows_d, rows_e)
    sixth, low_active1, low_grads1, scaled, rows = lax.optimization_barrier(
        (sixth, low_active1, low_grads1, scaled, rows)
    )
    active = both(top_active0, top_active1, low_active0, low_active1)
    grads = both(top_grads0, top_grads1, low_grads0, low_grads1)
    other_up = swap(dot(rows, grads[:, hidden:], over).astype(BF), "dp")
    other_down = swap(dot(active[:, hidden:], scaled, over).astype(BF), "dp")
    grad_up = (dot(rows, grads[:, :hidden], over) + other_up.astype(F32)).astype(BF)
    grad_down = (dot(active[:, :hidden], scaled, over) + other_down.astype(F32)).astype(BF)
    grad_up, grad_down = cross(grad_up), cross(grad_down)
    seventh, grad_up, grad_down = lax.optimization_barrier((seventh, grad_up, grad_down))
    low_out0 = combine(sixth, unpacker, place_t[0], (low_in0, ()))
    low_out1 = combine(seventh, unpacker, place_t[1], (low_in1, ()))
    results = jnp.stack([pick(top_out0, low_out0), pick(top_out1, low_out1)])
    return results[None], grad_up[None, None], grad_down[None, None]


def solution(mesh):
    sizes = dict(zip(mesh.axis_names, mesh.devices.shape))
    fine = Mesh(
        mesh.devices.reshape(sizes["section"], sizes["dp"], sizes["expert"] // 2, 2),
        ("section", "dp", "pair", "half"),
    )
    tokens = P("section", None, ("dp", "pair", "half"), None)
    up, down = P("section", PAIRED, "dp", None), P("section", PAIRED, None, "dp")
    return jax.shard_map(
        on_device,
        mesh=fine,
        in_specs=(P(None, ("dp", "pair", "half"), None), tokens, tokens, tokens, up, down),
        out_specs=(tokens, up, down),
        check_vma=False,
    )
```

```python
import functools

import jax
import jax.numpy as jnp
from jax import lax
from jax.experimental import pallas as pl
from jax.experimental.pallas import tpu as pltpu
from jax.sharding import Mesh, PartitionSpec as P

BF = jnp.bfloat16
F32 = jnp.float32
LANES = 128
GROUP = 16
VMEM_BYTES = 28 << 20
CAP = 5
PAIRED = ("pair", "half")
ROWS = GROUP * CAP
NT = (((1,), (1,)), ((), ()))


def vmem_call(body, outs, scratch=(), scalars=0):
    spec = pl.BlockSpec(memory_space=pltpu.VMEM)
    smem = pl.BlockSpec(memory_space=pltpu.SMEM)

    def call(*args):
        return pl.pallas_call(
            body,
            out_shape=outs,
            in_specs=[smem] * scalars + [spec] * (len(args) - scalars),
            out_specs=jax.tree.map(lambda _: spec, outs),
            scratch_shapes=list(scratch),
            cost_estimate=pl.CostEstimate(flops=1, bytes_accessed=1, transcendentals=0),
            compiler_params=pltpu.CompilerParams(vmem_limit_bytes=VMEM_BYTES),
        )(*args)

    return call


def dot(a, b, dims=(((1,), (0,)), ((), ()))):
    return lax.dot_general(a, b, dims, preferred_element_type=F32)


def pack(source, starts, pack_ref, mixed, store):
    blocks = mixed.shape[0] // ROWS
    for side, (row, col) in enumerate(starts):
        for block in range(blocks):
            mixed[block * ROWS : (block + 1) * ROWS, side * LANES : (side + 1) * LANES] = source[
                row : row + ROWS, col + block * LANES : col + (block + 1) * LANES
            ]
    chunks = dot(pack_ref[...], mixed[...])
    high = chunks.shape[0] // GROUP
    for side in range(2):
        for item in range(GROUP):
            store(
                side,
                item,
                chunks[item * high : (item + 1) * high, side * LANES : (side + 1) * LANES].astype(BF),
            )


def unpack(load, unpack_ref, stage, target, starts):
    high = stage.shape[0] // GROUP
    for side in range(2):
        for item in range(GROUP):
            stage[item * high : (item + 1) * high, side * LANES : (side + 1) * LANES] = load(side, item).astype(F32)
    mixed = dot(unpack_ref[...], stage[...].astype(BF))
    for side, (row, col) in enumerate(starts):
        for block in range(mixed.shape[0] // ROWS):
            target[row : row + ROWS, col + block * LANES : col + (block + 1) * LANES] = mixed[
                block * ROWS : (block + 1) * ROWS, side * LANES : (side + 1) * LANES
            ].astype(BF)


def dispatch_body(count, *refs):
    values, places, weights = refs[:count], refs[count : 2 * count], refs[2 * count : 3 * count]
    pack_ref, out, slots, mixed = refs[3 * count :]
    half = slots.shape[1] // 2
    for index in range(count):
        slots[...] = (dot(places[index][...], values[index][...]) * weights[index][...]).astype(BF)
        for group in range(slots.shape[0] // ROWS):

            def store(side, item, chunk, index=index, group=group):
                out[(group * GROUP + item) * 2 + side, index] = chunk

            pack(slots, [(group * ROWS, 0), (group * ROWS, half)], pack_ref, mixed, store)


def dispatch(values, places, weights, packer, chunk_rows):
    count = len(values)
    slot_count, width = places[0].shape[0], values[0].shape[1]
    experts = slot_count // CAP
    return vmem_call(
        functools.partial(dispatch_body, count),
        jax.ShapeDtypeStruct((2 * experts, count, chunk_rows, LANES), BF),
        [pltpu.VMEM((slot_count, width), BF), pltpu.VMEM((packer.shape[1], 2 * LANES), BF)],
    )(*values, *places, *weights, packer)


def unpack_all(got, index, unpack_ref, stage, rows):
    for pair in range(got.shape[0] // (2 * GROUP)):

        def load(side, item, pair=pair):
            return got[(2 * pair + side) * GROUP + item, index]

        unpack(load, unpack_ref, stage, rows, [(2 * pair * ROWS, 0), ((2 * pair + 1) * ROWS, 0)])


def by_parts(rows, parts, dims, own, sent):
    start = 0
    for part in parts:
        product = dot(rows[...], part[...], dims)
        width = product.shape[1]
        own[:, start : start + width] = product
        sent[:, start : start + width] = product.astype(BF)
        start += width


def arrive_body(index, got, unpack_ref, part0, part1, rows, own, sent, stage):
    unpack_all(got, index, unpack_ref, stage, rows)
    dims = NT if part0.shape[1] == rows.shape[1] else (((1,), (0,)), ((), ()))
    by_parts(rows, (part0, part1), dims, own, sent)


def arrive_either_body(index, flag, got, unpack_ref, up0, up1, down0, down1, rows, own, sent, stage):
    unpack_all(got, index, unpack_ref, stage, rows)

    @pl.when(flag[0] == 1)
    def _():
        by_parts(rows, (down0, down1), NT, own, sent)

    @pl.when(flag[0] == 0)
    def _():
        by_parts(rows, (up0, up1), (((1,), (0,)), ((), ())), own, sent)


def shapes_of(got, hidden, width):
    total = got.shape[0] * CAP
    return (
        jax.ShapeDtypeStruct((total, width), BF),
        jax.ShapeDtypeStruct((total, hidden), F32),
        jax.ShapeDtypeStruct((total, hidden), BF),
    )


def arrive(got, index, unpacker, parts):
    stage = pltpu.VMEM((unpacker.shape[1], 2 * LANES), F32)
    hidden = 2 * min(parts[0].shape)
    return vmem_call(functools.partial(arrive_body, index), shapes_of(got, hidden, max(parts[0].shape)), [stage])(
        got, unpacker, *parts
    )


def arrive_either(flag, got, index, unpacker, ups, downs):
    stage = pltpu.VMEM((unpacker.shape[1], 2 * LANES), F32)
    return vmem_call(
        functools.partial(arrive_either_body, index),
        shapes_of(got, 2 * ups[0].shape[1], ups[0].shape[0]),
        [stage],
        1,
    )(flag, got, unpacker, *ups, *downs)


def turn_body(pre_own, pre_got, act_own, act_got, up0, up1, pack_ref, active, grads, out, rows, mixed):
    pre = pre_own[...] + pre_got[...].astype(F32)
    gate = 1.0 / (1.0 + jnp.exp(-pre))
    active[...] = (pre * gate).astype(BF)
    slope = gate * (1.0 + pre * (1.0 - gate))
    grads[...] = ((act_own[...] + act_got[...].astype(F32)) * slope).astype(BF)
    hidden = up0.shape[1]
    rows[...] = (dot(grads[:, :hidden], up0[...], NT) + dot(grads[:, hidden:], up1[...], NT)).astype(BF)
    for pair in range(out.shape[0] // (2 * GROUP)):

        def store(side, item, chunk, pair=pair):
            out[(2 * pair + side) * GROUP + item, 0] = chunk

        pack(rows, [(2 * pair * ROWS, 0), ((2 * pair + 1) * ROWS, 0)], pack_ref, mixed, store)


def turn(pre_own, pre_got, act_own, act_got, ups, packer, chunk_rows):
    total, hidden = pre_own.shape
    width = ups[0].shape[0]
    kept = jax.ShapeDtypeStruct((total, hidden), BF)
    return vmem_call(
        turn_body,
        (kept, kept, jax.ShapeDtypeStruct((total // CAP, 1, chunk_rows, LANES), BF)),
        [pltpu.VMEM((total, width), BF), pltpu.VMEM((packer.shape[1], 2 * LANES), BF)],
    )(pre_own, pre_got, act_own, act_got, *ups, packer)


def combine_body(got, unpack_ref, place_t, incoming, out, slots, stage):
    half = slots.shape[1] // 2
    for group in range(slots.shape[0] // ROWS):

        def load(side, item, group=group):
            return got[(group * GROUP + item) * 2 + side, 0]

        unpack(load, unpack_ref, stage, slots, [(group * ROWS, 0), (group * ROWS, half)])
    out[...] = (dot(place_t[...], slots[...]) + incoming[...].astype(F32)).astype(BF)


def combine(got, unpacker, place_t, incoming):
    return vmem_call(
        combine_body,
        jax.ShapeDtypeStruct(incoming.shape, BF),
        [
            pltpu.VMEM((place_t.shape[1], incoming.shape[1]), BF),
            pltpu.VMEM((unpacker.shape[1], 2 * LANES), F32),
        ],
    )(got, unpacker, place_t, incoming)


def slots_of(routes, gates, experts):
    tokens, top = routes.shape
    flat = routes.reshape(-1)
    order = jnp.arange(tokens * top, dtype=jnp.int32)
    earlier = (flat[:, None] == flat[None, :]) & (order[None, :] < order[:, None])
    slot = flat * CAP + jnp.sum(earlier.astype(jnp.int32), axis=1)
    hits = slot.reshape(tokens, top)[None] == jnp.arange(experts * CAP, dtype=jnp.int32)[:, None, None]
    place = jnp.any(hits, axis=2)
    weight = jnp.sum(jnp.where(hits, gates[None], 0.0), axis=(1, 2))
    return place.astype(BF), weight[:, None]


def packing(blocks, chunk_rows):
    total = GROUP * chunk_rows
    row = jnp.arange(total, dtype=jnp.int32)
    col = jnp.arange(blocks * ROWS, dtype=jnp.int32)
    item, place = row // chunk_rows, row % chunk_rows
    block, inner = place // CAP, place % CAP
    wanted = jnp.where(block < blocks, block * ROWS + item * CAP + inner, -1)
    return (wanted[:, None] == col[None, :]).astype(BF), (wanted[None, :] == col[:, None]).astype(BF)


def swap(value, axis):
    return lax.ppermute(value, axis, [(0, 1), (1, 0)])


def cross(value):
    moved = lax.ppermute(value, ("dp", "half"), [(1, 2), (2, 1)])
    return jnp.where(lax.axis_index("dp") == lax.axis_index("half"), value, moved)


def send(chunks):
    return lax.all_to_all(chunks, PAIRED, split_axis=0, concat_axis=0, tiled=True)


def on_device(grad_out, layer_in, routes, gates, w_up, w_down):
    section = lax.axis_index("section")
    top_section = section == lax.axis_size("section") - 1
    flag = top_section.astype(jnp.int32)[None]
    experts = lax.axis_size("pair")
    width = grad_out.shape[2]
    blocks = width // (2 * LANES)
    chunk_rows = -(-blocks * CAP // 8) * 8
    packer, unpacker = packing(blocks, chunk_rows)

    place, weight = zip(*[slots_of(routes[0, micro], gates[0, micro], experts) for micro in range(2)])
    place_t = [p.T for p in place]
    ones = jnp.ones_like(weight[0])
    inputs = [layer_in[0, 0], layer_in[0, 1]]

    up_here, down_here = cross(w_up[0, 0]), cross(w_down[0, 0])
    ups = (up_here, swap(up_here, "dp"))
    downs = (down_here, swap(down_here, "dp"))

    def pick(here, there):
        return jnp.where(top_section, here, there)

    def prepare(values, places, weights):
        return dispatch(values, places, weights, packer, chunk_rows)

    def top_start():
        first = send(prepare([inputs[0], grad_out[0]], [place[0]] * 2, [ones, weight[0]]))
        return first, prepare([inputs[1], grad_out[1]], [place[1]] * 2, [ones, weight[1]])

    def low_start():
        chunks = prepare(inputs, place, [ones, ones])
        return jnp.zeros_like(chunks), chunks

    first, second_chunks = lax.cond(top_section, top_start, low_start)
    first, second_chunks, unpacker = lax.optimization_barrier((first, second_chunks, unpacker))
    second = send(second_chunks)

    rows_a0, own_a0, sent_a0 = arrive(first, 0, unpacker, ups)
    got_a0 = swap(sent_a0, "half")
    rows_a1, own_a1, sent_a1 = arrive(first, 1, unpacker, downs)
    got_a1 = swap(sent_a1, "half")
    top_active0, top_grads0, back0 = turn(own_a0, got_a0, own_a1, got_a1, ups, packer, chunk_rows)
    second, back0 = lax.optimization_barrier((second, back0))
    third = send(back0)

    rows_b0, own_b0, sent_b0 = arrive(second, 0, unpacker, ups)
    got_b0 = swap(sent_b0, "half")
    rows_b1, own_b1, sent_b1 = arrive_either(flag, second, 1, unpacker, ups, downs)
    got_b1 = swap(sent_b1, "half")
    top_active1, top_grads1, back1 = turn(own_b0, got_b0, own_b1, got_b1, ups, packer, chunk_rows)

    top_out0 = combine(third, unpacker, place_t[0], grad_out[0])
    low_in0 = lax.ppermute(top_out0, "section", [(1, 0)])
    fourth_chunks = pick(back1, dispatch([low_in0], [place[0]], [weight[0]], packer, chunk_rows))
    rows_in0, rows_in1 = pick(rows_a0, rows_b0), pick(rows_b0, rows_b1)
    fourth = send(fourth_chunks)
    top_out1 = combine(fourth, unpacker, place_t[1], grad_out[1])
    low_in1 = lax.ppermute(top_out1, "section", [(1, 0)])
    rows_d, own_d, sent_d = arrive(fourth, 0, unpacker, downs)
    low_in1, sent_d = lax.optimization_barrier((low_in1, sent_d))
    got_d = swap(sent_d, "half")

    fifth = send(dispatch([low_in1], [place[1]], [weight[1]], packer, chunk_rows))
    low_active0, low_grads0, back2 = turn(own_b0, got_b0, own_d, got_d, ups, packer, chunk_rows)
    fifth, back2 = lax.optimization_barrier((fifth, back2))
    rows_e, own_e, sent_e = arrive(fifth, 0, unpacker, downs)
    sent_e, back2 = lax.optimization_barrier((sent_e, back2))
    got_e = swap(sent_e, "half")
    sixth = send(back2)
    low_active1, low_grads1, back3 = turn(own_b1, got_b1, own_e, got_e, ups, packer, chunk_rows)
    seventh = send(back3)

    def both(top0, top1, low0, low1):
        return jnp.concatenate([pick(top0, low0), pick(top1, low1)])

    hidden = own_a0.shape[1] // 2
    over = (((0,), (0,)), ((), ()))
    rows = jnp.concatenate([rows_in0, rows_in1])
    scaled = both(rows_a1, rows_b1, rows_d, rows_e)
    sixth, low_active1, low_grads1, scaled, rows = lax.optimization_barrier(
        (sixth, low_active1, low_grads1, scaled, rows)
    )
    active = both(top_active0, top_active1, low_active0, low_active1)
    grads = both(top_grads0, top_grads1, low_grads0, low_grads1)
    other_up = swap(dot(rows, grads[:, hidden:], over).astype(BF), "dp")
    other_down = swap(dot(active[:, hidden:], scaled, over).astype(BF), "dp")
    grad_up = (dot(rows, grads[:, :hidden], over) + other_up.astype(F32)).astype(BF)
    grad_down = (dot(active[:, :hidden], scaled, over) + other_down.astype(F32)).astype(BF)
    grad_up, grad_down = cross(grad_up), cross(grad_down)
    seventh, grad_up, grad_down = lax.optimization_barrier((seventh, grad_up, grad_down))
    low_out0 = combine(sixth, unpacker, place_t[0], low_in0)
    low_out1 = combine(seventh, unpacker, place_t[1], low_in1)
    results = jnp.stack([pick(top_out0, low_out0), pick(top_out1, low_out1)])
    return results[None], grad_up[None, None], grad_down[None, None]


def solution(mesh):
    sizes = dict(zip(mesh.axis_names, mesh.devices.shape))
    fine = Mesh(
        mesh.devices.reshape(sizes["section"], sizes["dp"], sizes["expert"] // 2, 2),
        ("section", "dp", "pair", "half"),
    )
    tokens = P("section", None, ("dp", "pair", "half"), None)
    up, down = P("section", PAIRED, "dp", None), P("section", PAIRED, None, "dp")
    return jax.shard_map(
        on_device,
        mesh=fine,
        in_specs=(P(None, ("dp", "pair", "half"), None), tokens, tokens, tokens, up, down),
        out_specs=(tokens, up, down),
        check_vma=False,
    )
```
